32 devices in a mesh: row: 8 (over z, x), col: 2 (over y), rep: 2 (over core).
Axes of the slice: x: 2, y: 2, z: 4, core: 2. Of those that a mesh axis runs over, the one named last changes fastest.
Arguments:
- basis: bfloat16 [64, 1024, 128], P('row', None, 'rep'), may hold values from -6 to 6
- tiles: bfloat16 [8, 2, 4, 1024, 1024], P('row', 'col'), may hold values from -1.5 to 1.5
- slots: int32 [8, 2, 4, 2], P('row', 'col'), may hold values from -1 to 63, as said below
- sectors: int32 [64, 1024], replicated, may hold values from 0 to 10
Outputs:
- next_basis: float32 [64, 1024, 128], P('row', 'col', 'rep')
- projected: float32 [2, 128, 128], replicated
The draws below stay inside these ranges and needn't reach their ends.
Inputs may be any that keep to these rules, and one draw needn't show every extreme that they name: For owner (r, c), the first two indices of slots, each live slot holds (I, J) with 8 * r <= I < 8 * (r + 1) and 32 * c <= J < 32 * (c + 1). Live slots come first, every owner has at least one, an empty slot holds (-1, -1). Each pair of block indices, in either order, is held by one live slot at most among all owners. At most 4 live slots an owner, and some owner has all 4 live.
All inputs are finite; a program needn't handle non-finite values.
Results may differ from the reference program's by a relative error of at most 0.0025.
Values may be sent and summed in bfloat16 or wider, within the bound.
A program may use at most 128 MiB of HBM per device.

```python
import jax
import jax.numpy as jnp
from jax import lax

B = 1024
K = 128
NSEC = 11
TPD = 4
PRODUCTS = 2
BPR = 8
NB = 64
ASSETS = 65536
N_ROW = 8
N_COL = 2


def draw_slots(key, part):
    owners = N_ROW * N_COL
    col_blocks = BPR * (N_ROW // N_COL)
    places = BPR * col_blocks
    position = jnp.arange(places, dtype=jnp.int32)[None, None, :]
    owner_rows = jnp.arange(N_ROW, dtype=jnp.int32)[:, None, None]
    owner_cols = jnp.arange(N_COL, dtype=jnp.int32)[None, :, None]
    block_rows = jnp.broadcast_to(owner_rows * BPR + position // col_blocks, (N_ROW, N_COL, places))
    block_cols = jnp.broadcast_to(owner_cols * col_blocks + position % col_blocks, (N_ROW, N_COL, places))
    parity = (block_rows + block_cols) % 2 == 0
    allowed = (block_rows == block_cols) | ((block_rows < block_cols) == parity)
    score_key, count_key, pick_key = jax.random.split(key, 3)
    scores = jax.random.randint(score_key, (N_ROW, N_COL, places), 0, 4096) * places + position
    scores = jnp.where(allowed, scores, -1 - position)
    order = jnp.argsort(-scores, axis=-1, stable=True)[:, :, :TPD]
    chosen_rows = jnp.take_along_axis(block_rows, order, axis=-1)
    chosen_cols = jnp.take_along_axis(block_cols, order, axis=-1)
    levels = jax.random.randint(count_key, (N_ROW, N_COL), 0, 16)
    counts = jnp.where(levels < 8, 1, jnp.where(levels < 12, 2, jnp.where(levels < 14, 3, 4)))
    counts = jnp.minimum(counts, TPD).reshape(-1)
    fullest = jax.random.randint(pick_key, (), 0, owners)
    counts = counts.at[fullest].set(TPD).reshape(N_ROW, N_COL)
    live_slot = jnp.arange(TPD, dtype=jnp.int32)[None, None, :] < counts[:, :, None]
    live_rows = jnp.where(live_slot, chosen_rows, -1)
    live_cols = jnp.where(live_slot, chosen_cols, -1)
    return jnp.stack([live_rows, live_cols], axis=-1).astype(jnp.int32)


def place_ends(result, stream_key, low, top_value):
    longest = result.shape.index(max(result.shape))
    spots = []
    for shift in (0, 1):
        where = [jax.random.randint(jax.random.fold_in(stream_key, axis), (), 0, length) for axis, length in enumerate(result.shape)]
        where[longest] = (where[longest] + shift) % result.shape[longest]
        spots.append(tuple(where))
    return result.at[spots[0]].set(low).at[spots[1]].set(top_value)


def level_of(own_key, extent, pieces, smallest, high):
    factor_of = 1.0
    for axis_at, parts in pieces:
        draws = jax.random.uniform(jax.random.fold_in(jax.random.fold_in(own_key, 6), axis_at), (parts,), jnp.float32, smallest / len(pieces), high / len(pieces))
        factor_of = factor_of * jnp.repeat(jnp.exp(draws), extent[axis_at] // parts).reshape((-1,) + (1,) * (len(extent) - 1 - axis_at))
    return factor_of


def gaussian(rng, shape, spread, most, cuts=(), kind=jnp.bfloat16):
    factor_of = level_of(rng, shape, cuts, -0.22, 0.18) if cuts else 1.0
    result = jax.random.normal(rng, shape, jnp.float32) * spread * factor_of
    return jnp.minimum(jnp.maximum(result, -most), most).astype(kind)


def setup_inputs(seed: int = 0) -> dict:
    keys = jax.random.split(jax.random.key(seed), 5)
    basis = gaussian(keys[0], (NB, B, K), 1.0, 6.0, ((0, 8), (2, 2)))
    tiles = gaussian(keys[1], (N_ROW, N_COL, TPD, B, B), ((NSEC * BPR / (4 * N_COL * B)) ** 0.5), 1.5, ((0, 8), (1, 2)))
    slots = draw_slots(jax.random.fold_in(keys[4], 71), 0)
    sectors = place_ends(jax.random.randint(keys[3], (NB, B), 0, NSEC), jax.random.fold_in(keys[3], 1), 0, NSEC - 1).astype(jnp.int32)
    return dict(basis=basis, tiles=tiles, slots=slots, sectors=sectors)


def multiply(current, tile_stack, slot_pairs, sectors):

    def visit_tile(totals, tile_entry):
        one_tile, slot_pair = tile_entry
        block_row = jnp.maximum(slot_pair[0], 0).astype(jnp.int32)
        block_col = jnp.maximum(slot_pair[1], 0).astype(jnp.int32)
        row_sector = lax.dynamic_index_in_dim(sectors, block_row, 0, keepdims=False)
        col_sector = lax.dynamic_index_in_dim(sectors, block_col, 0, keepdims=False)
        keep_entry = (row_sector[:, None] == col_sector[None, :]) & (slot_pair[0] >= 0)
        masked = jnp.where(keep_entry, one_tile, jnp.zeros((), one_tile.dtype))
        col_input = lax.dynamic_index_in_dim(current, block_col, 0, keepdims=False)
        row_input = lax.dynamic_index_in_dim(current, block_row, 0, keepdims=False)
        forward = jnp.dot(masked.astype(jnp.float32), col_input.astype(jnp.float32), preferred_element_type=jnp.float32)
        backward = jnp.dot(masked.T.astype(jnp.float32), row_input.astype(jnp.float32), preferred_element_type=jnp.float32)
        totals = totals.at[block_row].add(forward)
        totals = totals.at[block_col].add(backward)
        return (totals, None)
    initial = jnp.zeros(current.shape, jnp.float32)
    totals, unused = lax.scan(visit_tile, initial, (tile_stack, slot_pairs))
    return totals

def reference(basis, tiles, slots, sectors):
    tile_stack = tiles.reshape(-1, B, B)
    slot_pairs = slots.reshape(-1, 2)
    current = basis
    history = []
    solved = None
    for rounds in range(PRODUCTS):
        product = multiply(current, tile_stack, slot_pairs, sectors)
        values = product.reshape(ASSETS, K)
        previous = current.reshape(ASSETS, K).astype(jnp.float32)
        history.append(jnp.dot(previous.T, values, precision=lax.Precision.HIGHEST) / ASSETS)
        gram_matrix = jnp.dot(values.T, values, precision=lax.Precision.HIGHEST) / ASSETS
        factor = jnp.linalg.cholesky(gram_matrix)
        solved = jax.scipy.linalg.solve_triangular(factor, values.T, lower=True).T
        current = lax.optimization_barrier(solved.astype(jnp.bfloat16)).reshape(NB, B, K)
    return (solved.reshape(NB, B, K), jnp.stack(history))
```

```python
import jax
import jax.numpy as jnp
from jax import lax
from jax.sharding import PartitionSpec as P

PRODUCTS = 2


def projections(own_rows, previous, widened, rep_index, total_rows, full_cols):
    gram_block = jnp.dot(own_rows.T, widened, precision=lax.Precision.HIGHEST) / total_rows
    ritz_block = (
        jnp.dot(previous.astype(jnp.float32).T, widened, precision=lax.Precision.HIGHEST)
        / total_rows
    )
    zero_matrix = jnp.zeros((full_cols, full_cols), jnp.float32)
    row_start = rep_index * own_rows.shape[1]
    gram_part = lax.dynamic_update_slice_in_dim(zero_matrix, gram_block, row_start, 0)
    ritz_part = lax.dynamic_update_slice_in_dim(zero_matrix, ritz_block, row_start, 0)
    return (gram_part, ritz_part)


def solve_rows(gram_matrix, widened):
    factor = jnp.linalg.cholesky(gram_matrix)
    return jax.scipy.linalg.solve_triangular(factor, widened.T, lower=True).T


def body(basis, tiles, slots, sectors):
    row_count = lax.axis_size("row")
    col_count = lax.axis_size("col")
    row_index = lax.axis_index("row")
    col_index = lax.axis_index("col")
    rep_index = lax.axis_index("rep")
    blocks_here, tile_width, half_cols = basis.shape
    group_size = row_count // col_count
    col_blocks = blocks_here * group_size
    share_rows = tile_width // col_count
    total_rows = blocks_here * row_count * tile_width
    full_cols = half_cols * lax.axis_size("rep")
    slot_pairs = slots.reshape(-1, 2)
    tile_stack = tiles.reshape(-1, tile_width, tile_width)
    live_count = jnp.sum((slot_pairs[:, 0] >= 0).astype(jnp.int32))
    block_rows = jnp.maximum(slot_pairs[:, 0], 0)
    block_cols = jnp.maximum(slot_pairs[:, 1], 0)
    local_rows = jnp.clip(block_rows - blocks_here * row_index, 0, blocks_here - 1)
    local_cols = jnp.clip(block_cols - col_blocks * col_index, 0, col_blocks - 1)
    same_sector = sectors[block_rows][:, :, None] == sectors[block_cols][:, None, :]
    masked = jnp.where(same_sector, tile_stack, jnp.zeros((), tile_stack.dtype))
    row_panel = basis
    outcome = None
    history = []
    for rounds in range(PRODUCTS):
        whole_panel = lax.all_gather(row_panel, "row", axis=0, tiled=True)
        columns = lax.dynamic_slice_in_dim(whole_panel, col_index * col_blocks, col_blocks, 0)

        def accumulate(position, partials, columns=columns, row_panel=row_panel):
            row_totals, col_totals = partials
            one_tile = lax.dynamic_index_in_dim(masked, position, 0, keepdims=False)
            row_slot = local_rows[position]
            col_slot = local_cols[position]
            col_input = lax.dynamic_index_in_dim(columns, col_slot, 0, keepdims=False)
            row_input = lax.dynamic_index_in_dim(row_panel, row_slot, 0, keepdims=False)
            forward = jnp.dot(one_tile, col_input, preferred_element_type=jnp.float32)
            backward = lax.dot_general(
                one_tile, row_input, (((0,), (0,)), ((), ())), preferred_element_type=jnp.float32
            )
            return (row_totals.at[row_slot].add(forward), col_totals.at[col_slot].add(backward))

        initial = (jnp.zeros(row_panel.shape, jnp.float32), jnp.zeros(columns.shape, jnp.float32))
        row_part, col_part = lax.fori_loop(0, live_count, accumulate, initial)
        col_share = lax.psum_scatter(col_part, "row", scatter_dimension=1, tiled=True)
        col_total = lax.all_gather(col_share, "row", axis=1, tiled=True)
        own_block = lax.dynamic_slice_in_dim(
            col_total, row_index % group_size * blocks_here, blocks_here, 0
        )
        is_owner = row_index // group_size == col_index
        row_part = row_part + jnp.where(is_owner, own_block, jnp.zeros_like(own_block))
        summed = lax.psum(row_part, "col")
        own_rows = summed.reshape(-1, half_cols)
        previous = row_panel.reshape(-1, half_cols)
        widened = lax.all_gather(own_rows, "rep", axis=1, tiled=True)
        gram_part, ritz_part = projections(
            own_rows, previous, widened, rep_index, total_rows, full_cols
        )
        gram_matrix, ritz_matrix = lax.psum((gram_part, ritz_part), ("row", "rep"))
        solved = solve_rows(gram_matrix, widened)
        chosen = lax.dynamic_slice_in_dim(solved, rep_index * half_cols, half_cols, 1)
        next_block = chosen.reshape(blocks_here, tile_width, half_cols)
        outcome = lax.dynamic_slice_in_dim(next_block, col_index * share_rows, share_rows, 1)
        row_panel = lax.optimization_barrier(next_block.astype(jnp.bfloat16))
        history.append(ritz_matrix)
    return (outcome, jnp.stack(history))


def swap(value, axis, distance):
    count = lax.axis_size(axis)
    return lax.ppermute(value, axis, [(i, i ^ distance) for i in range(count)])


def swap_x(value):
    return swap(value, "row", 1)


def swap_low(value):
    return swap(value, "row", 2)


def swap_high(value):
    return swap(value, "row", 4)


def swap_col(value):
    return swap(value, "col", 1)


def swap_rep(value):
    return swap(value, "rep", 1)


def join(flag, first, second, axis):
    return jnp.where(
        flag == 0,
        jnp.concatenate([first, second], axis),
        jnp.concatenate([second, first], axis),
    )


def pick(blocks, places):
    count = blocks.shape[0]
    result = jnp.broadcast_to(blocks[0][None], places.shape + blocks.shape[1:])
    for block in range(1, count):
        result = jnp.where((places == block)[:, None, None], blocks[block][None], result)
    return result


def code(values):
    most = jnp.max(jnp.abs(values), axis=-1, keepdims=True)
    scale = jnp.where(most > 0, most * (1.0 / 32000.0), 1.0)
    return jnp.round(values / scale).astype(jnp.int16), scale


def decode(coded, scale):
    return coded.astype(jnp.float32) * scale


def place(values, targets, count):
    chosen = targets[None, :] == jnp.arange(count, dtype=jnp.int32)[:, None]
    total = jnp.zeros((count,) + values.shape[1:], jnp.float32)
    for n in range(values.shape[0]):
        total = total + jnp.where(chosen[:, n, None, None], values[n][None], 0.0)
    return total


def paired_body(basis, tiles, slots, sectors):
    row = lax.axis_index("row")
    col = lax.axis_index("col")
    rep = lax.axis_index("rep")
    blocks_here, width, half_cols = basis.shape
    share = width // 2
    total_rows = blocks_here * lax.axis_size("row") * width
    x, low, high = row % 2, row // 2 % 2, row // 4
    pairs = slots.reshape(-1, 2)
    slot_count = pairs.shape[0]
    is_home = col == high
    beside = swap_col(pairs)
    near = jnp.where(is_home, pairs, beside)
    far = swap_high(jnp.where(is_home, beside, pairs))
    low_pairs = swap_low(jnp.concatenate([near, far], 0))
    near_low, far_low = low_pairs[:slot_count], low_pairs[slot_count:]

    def spot(blocks):
        owner = blocks // blocks_here
        return (owner % 2 ^ x) * blocks_here + blocks % blocks_here, owner // 2 % 2

    wanted_spot, wanted_low = spot(jnp.concatenate([near[:, 1], far[:, 1]]))
    asked_spot, _ = spot(jnp.concatenate([near_low[:, 1], far_low[:, 1]]))
    wanted_spot = jnp.clip(wanted_spot, 0, 2 * blocks_here - 1)
    asked_spot = jnp.clip(asked_spot, 0, 2 * blocks_here - 1)
    own_rows = jnp.where(pairs[:, 0] >= 0, pairs[:, 0] - blocks_here * row, blocks_here)
    beside_rows = jnp.where(beside[:, 0] >= 0, beside[:, 0] - blocks_here * row, blocks_here)
    own_pick = jnp.clip(own_rows, 0, blocks_here - 1)
    beside_pick = jnp.clip(beside_rows, 0, blocks_here - 1)

    def target(blocks):
        at, at_low = spot(blocks)
        return jnp.where((blocks >= 0) & (at_low == low), at, -1)

    landing = jnp.concatenate(
        [target(each[:, 1]) for each in (near, far, near_low, far_low)]
    )

    block_rows = jnp.maximum(pairs[:, 0], 0)
    block_cols = jnp.maximum(pairs[:, 1], 0)

    def sector_rows(blocks):
        chosen = blocks[:, None] == jnp.arange(sectors.shape[0], dtype=jnp.int32)[None, :]
        return jnp.sum(jnp.where(chosen[:, :, None], sectors[None], 0), axis=1)

    keep = (sector_rows(block_rows)[:, :, None] == sector_rows(block_cols)[:, None, :]) & (
        pairs[:, 0] >= 0
    )[:, None, None]
    tile_stack = tiles.reshape(-1, width, width)
    masked = jnp.where(keep, tile_stack, jnp.zeros((), tile_stack.dtype))

    whole = jnp.swapaxes(basis, 1, 2)
    mine = lax.dynamic_slice_in_dim(whole, col * share, share, 2)
    row_input = pick(whole, own_pick)
    history = []
    solved = None
    for rounds in range(PRODUCTS):
        if rounds > 0:
            given = swap_col(pick(mine, beside_pick))
            row_input = join(col, pick(mine, own_pick), given, 2)
        batch = ((0,), (0,))
        backward = lax.dot_general(
            row_input, masked, (((2,), (1,)), batch), preferred_element_type=jnp.float32
        )
        held = jnp.concatenate([mine, swap_x(mine)], 0)
        arrived = swap_low(pick(held, asked_spot))
        here = (wanted_low == low)[:, None, None]
        found = jnp.where(here, pick(held, wanted_spot), arrived)
        crossed = swap_high(found[slot_count:])
        kept = found[:slot_count]
        half = jnp.where(is_home, kept, crossed)
        other = swap_col(jnp.where(is_home, crossed, kept))
        col_input = join(col, half, other, 2)

        coded, scale = code(backward)
        own_back = lax.dynamic_slice_in_dim(coded, col * share, share, 2)
        sent_back = lax.dynamic_slice_in_dim(coded, (1 - col) * share, share, 2)
        side_back, side_scale = swap_col(sent_back), swap_col(scale)
        stay = jnp.where(is_home, own_back, side_back)
        stay_scale = jnp.where(is_home, scale, side_scale)
        leave = jnp.where(is_home, side_back, own_back)
        leave_scale = jnp.where(is_home, side_scale, scale)
        gathered = jnp.concatenate([stay, swap_high(leave)], 0)
        gathered_scale = jnp.concatenate([stay_scale, swap_high(leave_scale)], 0)
        gathered = jnp.concatenate([gathered, swap_low(gathered)], 0)
        gathered_scale = jnp.concatenate([gathered_scale, swap_low(gathered_scale)], 0)
        values = decode(gathered, gathered_scale)
        away, away_scale = code(place(values, landing - blocks_here, blocks_here))
        away, away_scale = swap_x(away), swap_x(away_scale)
        back_total = place(values, landing, blocks_here) + decode(away, away_scale)

        forward = lax.dot_general(
            col_input, masked, (((2,), (2,)), batch), preferred_element_type=jnp.float32
        )
        forward_half = lax.dynamic_slice_in_dim(forward, col * share, share, 2)
        side_coded, side_scale = code(
            lax.dynamic_slice_in_dim(forward, (1 - col) * share, share, 2)
        )
        side_forward = decode(swap_col(side_coded), swap_col(side_scale))
        product = back_total + place(
            jnp.concatenate([forward_half, side_forward], 0),
            jnp.concatenate([own_rows, beside_rows]),
            blocks_here,
        )

        product = jnp.swapaxes(product, 0, 1).reshape(half_cols, -1)
        previous = jnp.swapaxes(mine, 0, 1).reshape(half_cols, -1).astype(jnp.float32)
        widened = join(rep, product, swap_rep(product), 0)
        sums = (
            lax.dot_general(
                jnp.concatenate([product, previous], 0),
                widened,
                (((1,), (1,)), ((), ())),
                precision=lax.Precision.HIGHEST,
            )
            / total_rows
        )
        for step in (swap_x, swap_low, swap_high, swap_col):
            sums = sums + step(sums)
        sums = sums.reshape(2, half_cols, -1)
        sums = join(rep, sums, swap_rep(sums), 1)
        history.append(sums[1])
        factor = jnp.linalg.cholesky(sums[0])
        inverse = jax.scipy.linalg.solve_triangular(
            factor, jnp.eye(factor.shape[0], dtype=jnp.float32), lower=True
        )
        chosen = lax.dynamic_slice_in_dim(inverse, rep * half_cols, half_cols, 0)
        solved = jnp.dot(chosen, widened, precision=lax.Precision.HIGHEST)
        solved = solved.reshape(half_cols, blocks_here, share)
        mine = lax.optimization_barrier(jnp.swapaxes(solved, 0, 1).astype(jnp.bfloat16))
    return (jnp.transpose(solved, (1, 2, 0)), jnp.stack(history))


def solution(mesh):
    placed = (
        P("row", None, "rep"),
        P("row", "col", None, None, None),
        P("row", "col", None, None),
        P(),
    )
    sizes = mesh.shape
    paired = sizes["row"] == 8 and sizes["col"] == 2 and sizes["rep"] == 2
    return jax.shard_map(
        paired_body if paired else body,
        mesh=mesh,
        in_specs=placed,
        out_specs=(P("row", "col", "rep"), P()),
        check_vma=False,
    )
```

```python
import jax
import jax.numpy as jnp
from jax import lax
from jax.experimental import pallas as pl
from jax.experimental.pallas import tpu as pltpu
from jax.sharding import PartitionSpec as P

PRODUCTS = 2


def projections(own_rows, previous, widened, rep_index, total_rows, full_cols):
    gram_block = jnp.dot(own_rows.T, widened, precision=lax.Precision.HIGHEST) / total_rows
    ritz_block = (
        jnp.dot(previous.astype(jnp.float32).T, widened, precision=lax.Precision.HIGHEST)
        / total_rows
    )
    zero_matrix = jnp.zeros((full_cols, full_cols), jnp.float32)
    row_start = rep_index * own_rows.shape[1]
    gram_part = lax.dynamic_update_slice_in_dim(zero_matrix, gram_block, row_start, 0)
    ritz_part = lax.dynamic_update_slice_in_dim(zero_matrix, ritz_block, row_start, 0)
    return (gram_part, ritz_part)


def solve_rows(gram_matrix, widened):
    factor = jnp.linalg.cholesky(gram_matrix)
    return jax.scipy.linalg.solve_triangular(factor, widened.T, lower=True).T


def body(basis, tiles, slots, sectors):
    row_count = lax.axis_size("row")
    col_count = lax.axis_size("col")
    row_index = lax.axis_index("row")
    col_index = lax.axis_index("col")
    rep_index = lax.axis_index("rep")
    blocks_here, tile_width, half_cols = basis.shape
    group_size = row_count // col_count
    col_blocks = blocks_here * group_size
    share_rows = tile_width // col_count
    total_rows = blocks_here * row_count * tile_width
    full_cols = half_cols * lax.axis_size("rep")
    slot_pairs = slots.reshape(-1, 2)
    tile_stack = tiles.reshape(-1, tile_width, tile_width)
    live_count = jnp.sum((slot_pairs[:, 0] >= 0).astype(jnp.int32))
    block_rows = jnp.maximum(slot_pairs[:, 0], 0)
    block_cols = jnp.maximum(slot_pairs[:, 1], 0)
    local_rows = jnp.clip(block_rows - blocks_here * row_index, 0, blocks_here - 1)
    local_cols = jnp.clip(block_cols - col_blocks * col_index, 0, col_blocks - 1)
    same_sector = sectors[block_rows][:, :, None] == sectors[block_cols][:, None, :]
    masked = jnp.where(same_sector, tile_stack, jnp.zeros((), tile_stack.dtype))
    row_panel = basis
    outcome = None
    history = []
    for rounds in range(PRODUCTS):
        whole_panel = lax.all_gather(row_panel, "row", axis=0, tiled=True)
        columns = lax.dynamic_slice_in_dim(whole_panel, col_index * col_blocks, col_blocks, 0)

        def accumulate(position, partials, columns=columns, row_panel=row_panel):
            row_totals, col_totals = partials
            one_tile = lax.dynamic_index_in_dim(masked, position, 0, keepdims=False)
            row_slot = local_rows[position]
            col_slot = local_cols[position]
            col_input = lax.dynamic_index_in_dim(columns, col_slot, 0, keepdims=False)
            row_input = lax.dynamic_index_in_dim(row_panel, row_slot, 0, keepdims=False)
            forward = jnp.dot(one_tile, col_input, preferred_element_type=jnp.float32)
            backward = lax.dot_general(
                one_tile, row_input, (((0,), (0,)), ((), ())), preferred_element_type=jnp.float32
            )
            return (row_totals.at[row_slot].add(forward), col_totals.at[col_slot].add(backward))

        initial = (jnp.zeros(row_panel.shape, jnp.float32), jnp.zeros(columns.shape, jnp.float32))
        row_part, col_part = lax.fori_loop(0, live_count, accumulate, initial)
        col_share = lax.psum_scatter(col_part, "row", scatter_dimension=1, tiled=True)
        col_total = lax.all_gather(col_share, "row", axis=1, tiled=True)
        own_block = lax.dynamic_slice_in_dim(
            col_total, row_index % group_size * blocks_here, blocks_here, 0
        )
        is_owner = row_index // group_size == col_index
        row_part = row_part + jnp.where(is_owner, own_block, jnp.zeros_like(own_block))
        summed = lax.psum(row_part, "col")
        own_rows = summed.reshape(-1, half_cols)
        previous = row_panel.reshape(-1, half_cols)
        widened = lax.all_gather(own_rows, "rep", axis=1, tiled=True)
        gram_part, ritz_part = projections(
            own_rows, previous, widened, rep_index, total_rows, full_cols
        )
        gram_matrix, ritz_matrix = lax.psum((gram_part, ritz_part), ("row", "rep"))
        solved = solve_rows(gram_matrix, widened)
        chosen = lax.dynamic_slice_in_dim(solved, rep_index * half_cols, half_cols, 1)
        next_block = chosen.reshape(blocks_here, tile_width, half_cols)
        outcome = lax.dynamic_slice_in_dim(next_block, col_index * share_rows, share_rows, 1)
        row_panel = lax.optimization_barrier(next_block.astype(jnp.bfloat16))
        history.append(ritz_matrix)
    return (outcome, jnp.stack(history))


def swap(value, axis, distance):
    count = lax.axis_size(axis)
    return lax.ppermute(value, axis, [(i, i ^ distance) for i in range(count)])


def swap_x(value):
    return swap(value, "row", 1)


def swap_low(value):
    return swap(value, "row", 2)


def swap_high(value):
    return swap(value, "row", 4)


def swap_col(value):
    return swap(value, "col", 1)


def swap_rep(value):
    return swap(value, "rep", 1)


def join(flag, first, second, axis):
    return jnp.where(
        flag == 0,
        jnp.concatenate([first, second], axis),
        jnp.concatenate([second, first], axis),
    )


def pick(blocks, places):
    count = blocks.shape[0]
    result = jnp.broadcast_to(blocks[0][None], places.shape + blocks.shape[1:])
    for block in range(1, count):
        result = jnp.where((places == block)[:, None, None], blocks[block][None], result)
    return result


def code(values):
    most = jnp.max(jnp.abs(values), axis=-1, keepdims=True)
    scale = jnp.where(most > 0, most * (1.0 / 32000.0), 1.0)
    return jnp.round(values / scale).astype(jnp.int16), scale


def decode(coded, scale):
    return coded.astype(jnp.float32) * scale


def place(values, targets, count):
    chosen = targets[None, :] == jnp.arange(count, dtype=jnp.int32)[:, None]
    total = jnp.zeros((count,) + values.shape[1:], jnp.float32)
    for n in range(values.shape[0]):
        total = total + jnp.where(chosen[:, n, None, None], values[n][None], 0.0)
    return total


STEP = 4


def factor_kernel(gram_ref, out_ref, work_ref):
    size = gram_ref.shape[0]
    row_ids = lax.broadcasted_iota(jnp.int32, (size, size), 0)
    col_ids = lax.broadcasted_iota(jnp.int32, (size, size), 1)
    work_ref[:, :size] = gram_ref[...]
    work_ref[:, size:] = jnp.where(row_ids == col_ids, 1.0, 0.0)
    lanes = lax.broadcasted_iota(jnp.int32, (1, size), 1)
    sides = lax.broadcasted_iota(jnp.int32, (size, 1), 0)

    def eliminate(block, carry):
        start = block * STEP
        left = work_ref[:, :size]
        rows = [work_ref[pl.ds(start + q, 1), :] for q in range(STEP)]
        columns = [
            jnp.sum(jnp.where(col_ids == start + q, left, 0.0), axis=1, keepdims=True)
            for q in range(STEP)
        ]
        pivots = [
            [
                jnp.sum(
                    jnp.where(lanes == start + p, rows[q][:, :size], 0.0), axis=1, keepdims=True
                )
                for p in range(q + 1)
            ]
            for q in range(STEP)
        ]
        factor = [[None] * STEP for _ in range(STEP)]
        upper, lower = [], []
        for q in range(STEP):
            row, column, diagonal = rows[q], columns[q], pivots[q][q]
            for p in range(q):
                value = pivots[q][p]
                for r in range(p):
                    value = value - factor[q][r] * factor[p][r]
                factor[q][p] = value * factor[p][p]
                diagonal = diagonal - factor[q][p] * factor[q][p]
                row = row - factor[q][p] * upper[p]
                column = column - factor[q][p] * lower[p]
            factor[q][q] = 1.0 / jnp.sqrt(diagonal)
            upper.append(row * factor[q][q])
            lower.append(column * factor[q][q])
        change = jnp.zeros(work_ref.shape, jnp.float32)
        below = sides >= start + STEP
        for q in range(STEP):
            change = change + jnp.where(below, lower[q], 0.0) * upper[q]
        work_ref[...] = work_ref[...] - change
        for q in range(STEP):
            work_ref[pl.ds(start + q, 1), :] = upper[q]
        return carry

    lax.fori_loop(0, size // STEP, eliminate, 0)
    out_ref[...] = work_ref[:, size:]


def inverse_factor(gram):
    size = gram.shape[0]
    return pl.pallas_call(
        factor_kernel,
        out_shape=jax.ShapeDtypeStruct((size, size), jnp.float32),
        in_specs=[pl.BlockSpec(memory_space=pltpu.VMEM)],
        out_specs=pl.BlockSpec(memory_space=pltpu.VMEM),
        scratch_shapes=[pltpu.VMEM((size, 2 * size), jnp.float32)],
    )(gram)


def paired_body(basis, tiles, slots, sectors):
    row = lax.axis_index("row")
    col = lax.axis_index("col")
    rep = lax.axis_index("rep")
    blocks_here, width, half_cols = basis.shape
    share = width // 2
    total_rows = blocks_here * lax.axis_size("row") * width
    x, low, high = row % 2, row // 2 % 2, row // 4
    pairs = slots.reshape(-1, 2)
    slot_count = pairs.shape[0]
    is_home = col == high
    beside = swap_col(pairs)
    near = jnp.where(is_home, pairs, beside)
    far = swap_high(jnp.where(is_home, beside, pairs))
    low_pairs = swap_low(jnp.concatenate([near, far], 0))
    near_low, far_low = low_pairs[:slot_count], low_pairs[slot_count:]

    def spot(blocks):
        owner = blocks // blocks_here
        return (owner % 2 ^ x) * blocks_here + blocks % blocks_here, owner // 2 % 2

    wanted_spot, wanted_low = spot(jnp.concatenate([near[:, 1], far[:, 1]]))
    asked_spot, _ = spot(jnp.concatenate([near_low[:, 1], far_low[:, 1]]))
    wanted_spot = jnp.clip(wanted_spot, 0, 2 * blocks_here - 1)
    asked_spot = jnp.clip(asked_spot, 0, 2 * blocks_here - 1)
    own_rows = jnp.where(pairs[:, 0] >= 0, pairs[:, 0] - blocks_here * row, blocks_here)
    beside_rows = jnp.where(beside[:, 0] >= 0, beside[:, 0] - blocks_here * row, blocks_here)
    own_pick = jnp.clip(own_rows, 0, blocks_here - 1)
    beside_pick = jnp.clip(beside_rows, 0, blocks_here - 1)

    def target(blocks):
        at, at_low = spot(blocks)
        return jnp.where((blocks >= 0) & (at_low == low), at, -1)

    landing = jnp.concatenate(
        [target(each[:, 1]) for each in (near, far, near_low, far_low)]
    )

    block_rows = jnp.maximum(pairs[:, 0], 0)
    block_cols = jnp.maximum(pairs[:, 1], 0)

    def sector_rows(blocks):
        chosen = blocks[:, None] == jnp.arange(sectors.shape[0], dtype=jnp.int32)[None, :]
        return jnp.sum(jnp.where(chosen[:, :, None], sectors[None], 0), axis=1)

    keep = (sector_rows(block_rows)[:, :, None] == sector_rows(block_cols)[:, None, :]) & (
        pairs[:, 0] >= 0
    )[:, None, None]
    tile_stack = tiles.reshape(-1, width, width)
    masked = jnp.where(keep, tile_stack, jnp.zeros((), tile_stack.dtype))

    whole = jnp.swapaxes(basis, 1, 2)
    mine = lax.dynamic_slice_in_dim(whole, col * share, share, 2)
    row_input = pick(whole, own_pick)
    history = []
    solved = None
    for rounds in range(PRODUCTS):
        if rounds > 0:
            given = swap_col(pick(mine, beside_pick))
            row_input = join(col, pick(mine, own_pick), given, 2)
        batch = ((0,), (0,))
        backward = lax.dot_general(
            row_input, masked, (((2,), (1,)), batch), preferred_element_type=jnp.float32
        )
        held = jnp.concatenate([mine, swap_x(mine)], 0)
        arrived = swap_low(pick(held, asked_spot))
        here = (wanted_low == low)[:, None, None]
        found = jnp.where(here, pick(held, wanted_spot), arrived)
        crossed = swap_high(found[slot_count:])
        kept = found[:slot_count]
        half = jnp.where(is_home, kept, crossed)
        other = swap_col(jnp.where(is_home, crossed, kept))
        col_input = join(col, half, other, 2)

        coded, scale = code(backward)
        own_back = lax.dynamic_slice_in_dim(coded, col * share, share, 2)
        sent_back = lax.dynamic_slice_in_dim(coded, (1 - col) * share, share, 2)
        side_back, side_scale = swap_col(sent_back), swap_col(scale)
        stay = jnp.where(is_home, own_back, side_back)
        stay_scale = jnp.where(is_home, scale, side_scale)
        leave = jnp.where(is_home, side_back, own_back)
        leave_scale = jnp.where(is_home, side_scale, scale)
        gathered = jnp.concatenate([stay, swap_high(leave)], 0)
        gathered_scale = jnp.concatenate([stay_scale, swap_high(leave_scale)], 0)
        gathered = jnp.concatenate([gathered, swap_low(gathered)], 0)
        gathered_scale = jnp.concatenate([gathered_scale, swap_low(gathered_scale)], 0)
        values = decode(gathered, gathered_scale)
        away, away_scale = code(place(values, landing - blocks_here, blocks_here))
        away, away_scale = swap_x(away), swap_x(away_scale)
        back_total = place(values, landing, blocks_here) + decode(away, away_scale)

        forward = lax.dot_general(
            col_input, masked, (((2,), (2,)), batch), preferred_element_type=jnp.float32
        )
        forward_half = lax.dynamic_slice_in_dim(forward, col * share, share, 2)
        side_coded, side_scale = code(
            lax.dynamic_slice_in_dim(forward, (1 - col) * share, share, 2)
        )
        side_forward = decode(swap_col(side_coded), swap_col(side_scale))
        product = back_total + place(
            jnp.concatenate([forward_half, side_forward], 0),
            jnp.concatenate([own_rows, beside_rows]),
            blocks_here,
        )

        product = jnp.swapaxes(product, 0, 1).reshape(half_cols, -1)
        previous = jnp.swapaxes(mine, 0, 1).reshape(half_cols, -1).astype(jnp.float32)
        widened = join(rep, product, swap_rep(product), 0)
        sums = (
            lax.dot_general(
                jnp.concatenate([product, previous], 0),
                widened,
                (((1,), (1,)), ((), ())),
                precision=lax.Precision.HIGHEST,
            )
            / total_rows
        )
        for step in (swap_x, swap_low, swap_high, swap_col):
            sums = sums + step(sums)
        sums = sums.reshape(2, half_cols, -1)
        sums = join(rep, sums, swap_rep(sums), 1)
        history.append(sums[1])
        inverse = inverse_factor(sums[0])
        chosen = lax.dynamic_slice_in_dim(inverse, rep * half_cols, half_cols, 0)
        solved = jnp.dot(chosen, widened, precision=lax.Precision.HIGHEST)
        solved = solved.reshape(half_cols, blocks_here, share)
        mine = lax.optimization_barrier(jnp.swapaxes(solved, 0, 1).astype(jnp.bfloat16))
    return (jnp.transpose(solved, (1, 2, 0)), jnp.stack(history))


def solution(mesh):
    placed = (
        P("row", None, "rep"),
        P("row", "col", None, None, None),
        P("row", "col", None, None),
        P(),
    )
    sizes = mesh.shape
    paired = sizes["row"] == 8 and sizes["col"] == 2 and sizes["rep"] == 2
    return jax.shard_map(
        paired_body if paired else body,
        mesh=mesh,
        in_specs=placed,
        out_specs=(P("row", "col", "rep"), P()),
        check_vma=False,
    )
```
